32 devices in a mesh: split: 8 (over z, y), group: 4 (over x, core).
Axes of the slice: x: 2, y: 2, z: 4, core: 2. Of those that a mesh axis runs over, the one named last changes fastest.
Arguments:
- field: float32 [128, 512, 512], P(('group', 'split')), parts along dimension 0, may hold values from -8 to 8
- selector: int32 [128], P('group'), parts along dimension 0, may hold values from 0 to 3
- profiles: float32 [16, 512], P('group'), parts along dimension 0, may hold values from 0.5 to 1.5
- row_gain: float32 [2048], P('group'), parts along dimension 0, may hold values from 0.5 to 1.5
- levels: int32 [16], P('group'), parts along dimension 0, may hold values from 5 to 7
Outputs:
- surplus: float32 [128, 512, 512], P(('group', 'split')), parts along dimension 0
The draws below stay inside these ranges and needn't reach their ends.
There are 4 independent parts, one for each index of `group`. The reference program is written for one: setup_inputs(seed, part) draws one part's arguments, and reference() takes and returns one part's arrays. A program takes and returns all parts, laid end to end along the dimension named above; each array names one. Nothing has to cross between parts.
All inputs are finite; a program needn't handle non-finite values.
Results may differ from the reference program's by a relative error of at most 0.00012.
Values sent between devices are 32-bit elements; how exact they have to be, the bound alone decides.
A program may use at most 192 MiB of HBM per device.

```python
import math
import jax
import jax.numpy as jnp

N2 = 512
N3 = 32
N4 = 16
FIELDS = 4
N1 = 32
N34 = 512


def draw_field(key, part):
    key = jax.random.fold_in(key, 11)
    return jnp.clip(jax.random.normal(key, (N1, N2, N3 * N4), jnp.float32), -6.0, 6.0)


def set_ends(drawn, rng, least, high):
    shape = drawn.shape
    index_at = [jax.random.randint(jax.random.fold_in(rng, axis), (), 0, shape[axis]) for axis in range(len(shape))]
    drawn = drawn.at[tuple(index_at)].set(least)
    longest = shape.index(max(shape))
    index_at[longest] = (index_at[longest] + 1) % shape[longest]
    return drawn.at[tuple(index_at)].set(high)


def setup_inputs(seed: int = 0, part: int = 0) -> dict:
    arg_keys = jax.random.split(jax.random.key(seed), 6)
    own_keys = jax.random.split(jax.random.fold_in(arg_keys[5], part), 6)
    field = draw_field(jax.random.fold_in(jax.random.fold_in(arg_keys[5], part), 71), part)
    selector = set_ends(jax.random.randint(own_keys[1], (N1,), 0, FIELDS), jax.random.fold_in(own_keys[1], 1), 0, FIELDS - 1).astype(jnp.int32)
    profiles = jnp.clip(jnp.exp(jax.random.uniform(own_keys[2], (FIELDS, N34), jnp.float32, math.log(0.5), math.log(1.5))), 0.5, 1.5)
    row_gain = jnp.clip(jnp.exp(jax.random.uniform(own_keys[3], (N2,), jnp.float32, math.log(0.5), math.log(1.5))), 0.5, 1.5)
    levels = set_ends(jax.random.randint(own_keys[4], (4,), 5, 8), jax.random.fold_in(own_keys[4], 1), 5, 7).astype(jnp.int32)
    return dict(field=field, selector=selector, profiles=profiles, row_gain=row_gain, levels=levels)


def lift_front(x):
    count = x.shape[0]
    stride = 1
    while stride < count:
        left = x[0::2 * stride]
        right = jnp.roll(left, -1, axis=0)
        x = x.at[stride::2 * stride].add(-0.5 * (left + right))
        stride = stride * 2
    return x


def lift_shifted(x):
    offset = x.shape[0] // 2
    return jnp.roll(lift_front(jnp.roll(x, offset, axis=0)), -offset, axis=0)


def lift_axis(x, axis):
    moved = jnp.moveaxis(x, axis, 0)
    return jnp.moveaxis(lift_front(moved), 0, axis)


def diffuse(ext_u, ext_a, weights):
    center = ext_u[1:-1]
    coef = ext_a[1:-1]

    def flux(u_next, u_prev, a_next, a_prev):
        return 0.5 * (coef + a_next) * (u_next - center) - 0.5 * (coef + a_prev) * (center - u_prev)

    position = jnp.arange(center.shape[2], dtype=jnp.int32) % N4

    def after(x):
        return jnp.where(position == N4 - 1, jnp.roll(x, N4 - 1, axis=2), jnp.roll(x, -1, axis=2))

    def before(x):
        return jnp.where(position == 0, jnp.roll(x, -(N4 - 1), axis=2), jnp.roll(x, 1, axis=2))

    first = flux(ext_u[2:], ext_u[:-2], ext_a[2:], ext_a[:-2])
    second = flux(jnp.roll(center, -1, axis=1), jnp.roll(center, 1, axis=1), jnp.roll(coef, -1, axis=1), jnp.roll(coef, 1, axis=1))
    third = flux(jnp.roll(center, -N4, axis=2), jnp.roll(center, N4, axis=2), jnp.roll(coef, -N4, axis=2), jnp.roll(coef, N4, axis=2))
    fourth = flux(after(center), before(center), after(coef), before(coef))
    return center + weights[0] * first + weights[1] * second + weights[2] * third + weights[3] * fourth


def axis_weights(levels):
    powers = jnp.exp2(levels.astype(jnp.float32))
    return 0.2 * powers / jnp.sum(powers)


def reference(field, selector, profiles, row_gain, levels):
    weights = axis_weights(levels)
    rows = profiles[selector]
    coef = rows[:, None, :] * row_gain[None, :, None]
    ext_u = jnp.concatenate([field[-1:], field, field[:1]], axis=0)
    ext_a = jnp.concatenate([coef[-1:], coef, coef[:1]], axis=0)
    diffused = diffuse(ext_u, ext_a, weights)
    result = lift_shifted(diffused)
    result = lift_axis(result, 1)
    shaped = result.reshape(result.shape[0], result.shape[1], N3, N4)
    shaped = lift_axis(shaped, 2)
    shaped = lift_axis(shaped, 3)
    return shaped.reshape(result.shape)
```

```python
import functools

import jax
import jax.numpy as jnp
import numpy as np
from jax import lax
from jax.experimental import pallas as pl
from jax.experimental.pallas import tpu as pltpu
from jax.sharding import PartitionSpec as P

N3 = 32
N4 = 16
CHUNKS = 8
STEP = 16
PAD = 8
HALF = 0.5


def low_bit(x):
    return x & -x


def lift_matrix(count):
    table = np.eye(count, dtype=np.float64)
    for j in range(1, count):
        s = low_bit(j)
        table[j, j - s] -= 0.5
        table[j, (j + s) % count] -= 0.5
    return table


def three_parts(x):
    high = x.astype(jnp.bfloat16)
    rest = x - high.astype(jnp.float32)
    middle = rest.astype(jnp.bfloat16)
    low = (rest - middle.astype(jnp.float32)).astype(jnp.bfloat16)
    return high, middle, low


def kernel(
    n,
    field,
    selector,
    profiles,
    row_gain,
    levels,
    second_table,
    merged_table,
    out,
    u,
    diffused,
    parts,
    lifted,
    result,
    f_prev,
    f_next,
    y_next,
    y_left,
    y_right,
    coefs,
    gains,
    local_sem,
    send_sem,
    recv_sem,
    out_sem,
):
    planes, rows, width = field.shape
    chunk = rows // CHUNKS
    me = lax.axis_index("split")
    total = n * planes
    rank = (me + n // 2) % n
    odd = me % 2 == 1
    even = me % 2 == 0
    ahead = (me + 1) % n
    behind = (me + n - 1) % n

    barrier = pltpu.get_barrier_semaphore()

    def greet(k, carry):
        pl.semaphore_signal(
            barrier,
            inc=1,
            device_id={"split": (me + k) % n},
            device_id_type=pl.DeviceIdType.MESH,
        )
        return carry

    lax.fori_loop(1, n, greet, 0)

    loads = [
        pltpu.make_async_copy(field, u.at[:, pl.ds(PAD, rows), :], local_sem.at[0]),
        pltpu.make_async_copy(
            field.at[:, pl.ds(rows - PAD, PAD), :], u.at[:, pl.ds(0, PAD), :], local_sem.at[1]
        ),
        pltpu.make_async_copy(
            field.at[:, pl.ds(0, PAD), :], u.at[:, pl.ds(rows + PAD, PAD), :], local_sem.at[2]
        ),
    ]
    for load in loads:
        load.start()

    def at(c):
        return pl.ds(pl.multiple_of(c * chunk, chunk), chunk)

    def remote(source, target, c, send, slot, device):
        return pltpu.make_async_remote_copy(
            src_ref=source,
            dst_ref=target.at[at(c), :],
            send_sem=send_sem.at[send, c],
            recv_sem=recv_sem.at[slot, c],
            device_id={"split": device},
            device_id_type=pl.DeviceIdType.MESH,
        )

    def last_plane(c):
        return remote(field.at[planes - 1, at(c), :], f_prev, c, 0, 0, ahead)

    def first_plane(c):
        return remote(field.at[0, at(c), :], f_next, c, 1, 1, behind)

    def own(c, target, send, slot, device):
        return remote(lifted.at[0, at(c), :], target, c, send, slot, device)

    def to_pair(c):
        return own(c, y_left, 2, 3, ahead)

    def to_behind(c):
        return own(c, y_next, 2, 2, behind)

    def relay(c):
        return remote(y_left.at[at(c), :], y_next, c, 3, 2, (me + n - 2) % n)

    sends = [(even, to_pair), (odd, to_behind)]
    s, slot = 2, 4
    while s < n:
        sends.append(
            (
                rank % (2 * s) == 0,
                functools.partial(
                    own, target=y_left, send=slot, slot=3, device=(me + s) % n
                ),
            )
        )
        if 2 * s < n:
            sends.append(
                (
                    rank % (2 * s) == 0,
                    functools.partial(
                        own, target=y_right, send=slot + 1, slot=4, device=(me + n - s) % n
                    ),
                )
            )
        s, slot = 2 * s, slot + 2

    pl.semaphore_wait(barrier, n - 1)

    def each(step):
        def body(c, carry):
            step(c)
            return carry

        lax.fori_loop(0, CHUNKS, body, 0)

    each(lambda c: last_plane(c).start())
    each(lambda c: first_plane(c).start())

    def power(d):
        return jnp.exp2(jnp.full((1, width), levels[d].astype(jnp.float32), jnp.float32))

    powers = [power(d) for d in range(4)]
    scale = 0.2 / (powers[0] + powers[1] + powers[2] + powers[3])
    w = [HALF * scale * power_d for power_d in powers]
    fields = profiles.shape[0]

    def profile(q):
        chosen = selector[(me * planes + q + total) % total]
        row = jnp.zeros((1, width), jnp.float32)
        for k in range(fields):
            row = row + jnp.where(chosen == k, profiles[pl.ds(k, 1), :], 0.0)
        return row

    lane = lax.broadcasted_iota(jnp.int32, (1, width), 1) % N4
    first_lane = lane == 0
    final_lane = lane == N4 - 1

    def shifted(x, by):
        return pltpu.roll(x, by % width, 1)

    def after(x):
        return jnp.where(final_lane, shifted(x, N4 - 1), shifted(x, -1))

    def before(x):
        return jnp.where(first_lane, shifted(x, 1 - N4), shifted(x, 1))

    chosen_rows = [profile(q) for q in range(-1, planes + 1)]
    for q in range(planes):
        low, mid, high = chosen_rows[q : q + 3]
        wide = jnp.broadcast_to(mid, (8, width))

        def pair(x):
            return (wide + x)[0:1]

        kinds = [
            w[0] * (mid + low),
            w[0] * (mid + high),
            w[2] * pair(shifted(wide, -N4)),
            w[2] * pair(shifted(wide, N4)),
            w[3] * pair(after(wide)),
            w[3] * pair(before(wide)),
            w[1] * mid,
        ]
        for k, row in enumerate(kinds):
            coefs[q, pl.ds(k, 1), :] = row
    gain = jnp.broadcast_to(row_gain[...], (128, rows))
    gains[0] = jnp.transpose(gain)
    gains[1] = jnp.transpose(gain + pltpu.roll(gain, rows - 1, 1))
    gains[2] = jnp.transpose(gain + pltpu.roll(gain, 1, 1))

    for load in loads:
        load.wait()

    def column(k, where):
        return jnp.concatenate([gains[k, where, :]] * (width // 128), axis=1)

    def diffuse(q, i):
        start = pl.multiple_of(i * STEP, STEP)
        here = pl.ds(start, STEP)
        inner = pl.ds(pl.multiple_of(start + PAD, 8), STEP)
        block = u[q, pl.ds(start, STEP + 2 * PAD), :]
        center = block[PAD : PAD + STEP]
        up = block[PAD - 1 : PAD - 1 + STEP]
        down = block[PAD + 1 : PAD + 1 + STEP]
        lower = u[jnp.maximum(q - 1, 0), inner, :]
        upper = u[jnp.minimum(q + 1, planes - 1), inner, :]

        def k(index):
            return coefs[q, pl.ds(index, 1), :]

        flow = k(0) * (lower - center) + k(1) * (upper - center)
        flow = flow + k(2) * (shifted(center, -N4) - center)
        flow = flow + k(3) * (shifted(center, N4) - center)
        flow = flow + k(4) * (after(center) - center) + k(5) * (before(center) - center)
        along = column(1, here) * (down - center) + column(2, here) * (up - center)
        diffused[q, here, :] = center + column(0, here) * flow + k(6) * along

    def join(q, c, index, other):
        def body(i, carry):
            start = pl.multiple_of(c * chunk + i * STEP, STEP)
            here = pl.ds(start, STEP)
            center = u[q, pl.ds(pl.multiple_of(start + PAD, 8), STEP), :]
            change = coefs[q, pl.ds(index, 1), :] * (other[here, :] - center)
            diffused[q, here, :] = diffused[q, here, :] + column(0, here) * change
            return carry

        lax.fori_loop(0, chunk // STEP, body, 0, unroll=True)

    def lift_lanes(q, c):
        where = at(c)
        total_ = jnp.zeros((chunk, width), jnp.float32)
        for part in reversed(three_parts(diffused[q, where, :])):
            total_ = total_ + jnp.dot(
                part, merged_table[...], preferred_element_type=jnp.float32
            )
        for k, part in enumerate(three_parts(total_)):
            parts[k, where, :] = part

    def lift_rows(q):
        block = min(128, rows)

        def body(i, carry):
            where = pl.ds(pl.multiple_of(i * block, block), block)
            table = second_table[where, :]
            total_ = jnp.dot(table, parts[2], preferred_element_type=jnp.float32)
            total_ = total_ + jnp.dot(table, parts[1], preferred_element_type=jnp.float32)
            total_ = total_ + jnp.dot(table, parts[0], preferred_element_type=jnp.float32)
            lifted[q, where, :] = total_
            return carry

        lax.fori_loop(0, rows // block, body, 0)

    def base(j, carry):
        diffuse(j // (rows // STEP), j % (rows // STEP))
        return carry

    lax.fori_loop(0, planes * (rows // STEP), base, 0, unroll=2)

    def inner_plane(q, carry):
        each(lambda c: lift_lanes(q, c))
        lift_rows(q)
        return carry

    lax.fori_loop(1, planes - 1, inner_plane, 0)

    def first_arrived(c):
        last_plane(c).wait_recv()
        join(0, c, 0, f_prev)
        lift_lanes(0, c)

    each(first_arrived)
    lift_rows(0)

    for holds, copy in sends:

        @pl.when(holds)
        def _(copy=copy):
            each(lambda c: copy(c).start())

    def last_arrived(c):
        first_plane(c).wait_recv()
        join(planes - 1, c, 1, f_next)
        lift_lanes(planes - 1, c)

    each(last_arrived)
    lift_rows(planes - 1)

    def store(q, c):
        return pltpu.make_async_copy(
            result.at[q, at(c), :], out.at[q, at(c), :], out_sem.at[q, c]
        )

    for q in range(1, planes):
        s = low_bit(q)
        if q + s < planes:

            def whole(c, q=q, s=s):
                where = at(c)
                result[q, where, :] = lifted[q, where, :] - HALF * (
                    lifted[q - s, where, :] + lifted[q + s, where, :]
                )
                store(q, c).start()

            each(whole)

    def finish(c):
        where = at(c)
        to_behind(c).wait_recv()
        for q in range(1, planes):
            s = low_bit(q)
            if q + s == planes:
                result[q, where, :] = lifted[q, where, :] - HALF * (
                    lifted[q - s, where, :] + y_next[where, :]
                )
                store(q, c).start()

        @pl.when(odd)
        def _():
            result[0, where, :] = lifted[0, where, :] - HALF * (
                y_left[where, :] + y_next[where, :]
            )

        @pl.when(rank == n // 2)
        def _():
            to_pair(c).wait_recv()
            result[0, where, :] = lifted[0, where, :] - y_left[where, :]

        @pl.when(rank == 0)
        def _():
            result[0, where, :] = lifted[0, where, :]

        @pl.when(even & (rank % (n // 2) != 0))
        def _():
            to_pair(c).wait_recv()
            own(c, y_right, 2, 4, ahead).wait_recv()
            result[0, where, :] = lifted[0, where, :] - HALF * (
                y_left[where, :] + y_right[where, :]
            )

        store(0, c).start()

    def pass_on(c):
        @pl.when(odd)
        def _():
            to_pair(c).wait_recv()
            relay(c).start()

    pass_on(0)

    def turn(c, carry):
        pass_on(c)
        finish(c - 1)
        return carry

    lax.fori_loop(1, CHUNKS, turn, 0)
    finish(CHUNKS - 1)

    each(lambda c: last_plane(c).wait_send())
    each(lambda c: first_plane(c).wait_send())
    for holds, copy in [*sends, (odd, relay)]:

        @pl.when(holds)
        def _(copy=copy):
            each(lambda c: copy(c).wait_send())

    for q in range(planes):
        each(lambda c, q=q: store(q, c).wait())


def on_device(field, selector, profiles, row_gain, levels):
    planes, rows, width = field.shape
    n = lax.axis_size("split")
    second_table = jnp.asarray(lift_matrix(rows).astype(jnp.bfloat16))
    merged_table = jnp.asarray(np.kron(lift_matrix(N3), lift_matrix(N4)).T.astype(jnp.bfloat16))
    kinds = 4 + 2 * n.bit_length()
    plane = pltpu.VMEM((rows, width), jnp.float32)
    block = pltpu.VMEM((planes, rows, width), jnp.float32)
    return pl.pallas_call(
        functools.partial(kernel, n),
        out_shape=jax.ShapeDtypeStruct(field.shape, jnp.float32),
        in_specs=[
            pl.BlockSpec(memory_space=pl.ANY),
            pl.BlockSpec(memory_space=pltpu.SMEM),
            pl.BlockSpec(memory_space=pltpu.VMEM),
            pl.BlockSpec(memory_space=pltpu.VMEM),
            pl.BlockSpec(memory_space=pltpu.SMEM),
            pl.BlockSpec(memory_space=pltpu.VMEM),
            pl.BlockSpec(memory_space=pltpu.VMEM),
        ],
        out_specs=pl.BlockSpec(memory_space=pl.ANY),
        scratch_shapes=[
            pltpu.VMEM((planes, rows + 2 * PAD, width), jnp.float32),
            block,
            pltpu.VMEM((3, rows, width), jnp.bfloat16),
            block,
            block,
            plane,
            plane,
            plane,
            plane,
            plane,
            pltpu.VMEM((planes, 8, width), jnp.float32),
            pltpu.VMEM((3, rows, 128), jnp.float32),
            pltpu.SemaphoreType.DMA((3,)),
            pltpu.SemaphoreType.DMA((kinds, CHUNKS)),
            pltpu.SemaphoreType.DMA((5, CHUNKS)),
            pltpu.SemaphoreType.DMA((planes, CHUNKS)),
        ],
        compiler_params=pltpu.CompilerParams(
            collective_id=0, has_side_effects=True, vmem_limit_bytes=50 * 1024 * 1024
        ),
        name="step_and_lift",
    )(
        field,
        selector,
        profiles,
        row_gain.reshape(1, rows),
        levels,
        second_table,
        merged_table,
    )


def solution(mesh):
    placed = (
        P(("group", "split"), None, None),
        P("group"),
        P("group", None),
        P("group"),
        P("group"),
    )
    return jax.shard_map(
        on_device,
        mesh=mesh,
        in_specs=placed,
        out_specs=P(("group", "split"), None, None),
        check_vma=False,
    )
```

```python
import functools

import jax
import jax.numpy as jnp
from jax import lax
from jax.experimental import pallas as pl
from jax.experimental.pallas import tpu as pltpu
from jax.sharding import PartitionSpec as P

N3 = 32
N4 = 16
CHUNKS = 4
STEP = 16
PAD = 8
HALF = 0.5
RELAY = True
LIMIT = 28


def low_bit(x):
    return x & -x


def lift_entries(j, k, count):
    s = low_bit(j)
    zero = jnp.zeros(j.shape, jnp.float32)
    less = jnp.where(k == j - s, HALF, zero) + jnp.where(k == ((j + s) & (count - 1)), HALF, zero)
    return jnp.where(j == k, 1.0, zero) - jnp.where(j == 0, zero, less)


def three_parts(x):
    high = x.astype(jnp.bfloat16)
    rest = x - high.astype(jnp.float32)
    middle = rest.astype(jnp.bfloat16)
    low = (rest - middle.astype(jnp.float32)).astype(jnp.bfloat16)
    return high, middle, low


def kernel(
    n,
    field,
    selector,
    profiles,
    row_gain,
    levels,
    out,
    u,
    diffused,
    parts,
    lifted,
    result,
    f_prev,
    f_next,
    y_next,
    y_left,
    y_right,
    coefs,
    gains,
    second_table,
    merged_table,
    local_sem,
    send_sem,
    recv_sem,
    out_sem,
):
    planes, rows, width = field.shape
    chunk = rows // CHUNKS
    me = lax.axis_index("split")
    total = n * planes
    rank = (me + n // 2) % n
    odd = me % 2 == 1
    even = me % 2 == 0
    ahead = (me + 1) % n
    behind = (me + n - 1) % n

    barrier = pltpu.get_barrier_semaphore()

    def greet(k, carry):
        pl.semaphore_signal(
            barrier,
            inc=1,
            device_id={"split": (me + k) % n},
            device_id_type=pl.DeviceIdType.MESH,
        )
        return carry

    lax.fori_loop(1, n, greet, 0)

    loads = [
        pltpu.make_async_copy(field, u.at[:, pl.ds(PAD, rows), :], local_sem.at[0]),
        pltpu.make_async_copy(
            field.at[:, pl.ds(rows - PAD, PAD), :], u.at[:, pl.ds(0, PAD), :], local_sem.at[1]
        ),
        pltpu.make_async_copy(
            field.at[:, pl.ds(0, PAD), :], u.at[:, pl.ds(rows + PAD, PAD), :], local_sem.at[2]
        ),
    ]
    for load in loads:
        load.start()

    def at(c):
        return pl.ds(pl.multiple_of(c * chunk, chunk), chunk)

    def remote(source, target, c, send, slot, device):
        return pltpu.make_async_remote_copy(
            src_ref=source,
            dst_ref=target.at[at(c), :],
            send_sem=send_sem.at[send, c],
            recv_sem=recv_sem.at[slot, c],
            device_id={"split": device},
            device_id_type=pl.DeviceIdType.MESH,
        )

    def last_plane(c):
        return remote(field.at[planes - 1, at(c), :], f_prev, c, 0, 0, ahead)

    def first_plane(c):
        return remote(field.at[0, at(c), :], f_next, c, 1, 1, behind)

    def own(c, target, send, slot, device):
        return remote(lifted.at[0, at(c), :], target, c, send, slot, device)

    def to_pair(c):
        return own(c, y_left, 2, 3, ahead)

    def to_behind(c):
        return own(c, y_next, 2, 2, behind)

    def relay(c):
        return remote(y_left.at[at(c), :], y_next, c, 3, 2, (me + n - 2) % n)

    def to_coarse(c):
        return remote(y_right.at[at(c), :], y_left, c, 2 + 2 * n.bit_length(), 3, behind_(n // 4))

    def to_opposite(c):
        return remote(
            y_left.at[at(c), :], y_right, c, 3 + 2 * n.bit_length(), 4, (me + n // 2) % n
        )

    def behind_(by):
        return (me + n - by) % n

    sends = [(even, to_pair), (odd, to_behind)]
    middle = me == n // 4
    s, slot = 2, 4
    while s < n // 2 if RELAY else s < n:
        sends.append(
            (
                rank % (2 * s) == 0,
                functools.partial(
                    own, target=y_left, send=slot, slot=3, device=(me + s) % n
                ),
            )
        )
        if 2 * s < n:
            holds = rank % (2 * s) == 0
            if RELAY and 4 * s == n:
                holds = rank == 0
            sends.append(
                (
                    holds,
                    functools.partial(
                        own, target=y_right, send=slot + 1, slot=4, device=(me + n - s) % n
                    ),
                )
            )
        s, slot = 2 * s, slot + 2

    pl.semaphore_wait(barrier, n - 1)

    def each(step):
        def body(c, carry):
            step(c)
            return carry

        lax.fori_loop(0, CHUNKS, body, 0)

    each(lambda c: last_plane(c).start())
    each(lambda c: first_plane(c).start())

    def grid(start, size):
        down = lax.broadcasted_iota(jnp.int32, (16, size), 0) + start
        return down, lax.broadcasted_iota(jnp.int32, (16, size), 1)

    def second_rows(i, carry):
        start = pl.multiple_of(i * 16, 16)
        j, k = grid(start, rows)
        second_table[pl.ds(start, 16), :] = lift_entries(j, k, rows).astype(jnp.bfloat16)
        return carry

    bits = N4.bit_length() - 1

    def merged_rows(i, carry):
        start = pl.multiple_of(i * 16, 16)
        k, j = grid(start, width)
        third = lift_entries(j >> bits, k >> bits, N3)
        fourth = lift_entries(j & (N4 - 1), k & (N4 - 1), N4)
        merged_table[pl.ds(start, 16), :] = (third * fourth).astype(jnp.bfloat16)
        return carry

    lax.fori_loop(0, rows // 16, second_rows, 0)
    lax.fori_loop(0, width // 16, merged_rows, 0)

    def power(d):
        return jnp.exp2(jnp.full((1, width), levels[d].astype(jnp.float32), jnp.float32))

    powers = [power(d) for d in range(4)]
    scale = 0.2 / (powers[0] + powers[1] + powers[2] + powers[3])
    w = [HALF * scale * power_d for power_d in powers]
    fields = profiles.shape[0]

    def profile(q):
        chosen = selector[(me * planes + q + total) % total]
        row = jnp.zeros((1, width), jnp.float32)
        for k in range(fields):
            row = row + jnp.where(chosen == k, profiles[pl.ds(k, 1), :], 0.0)
        return row

    lane = lax.broadcasted_iota(jnp.int32, (1, width), 1) % N4
    first_lane = lane == 0
    final_lane = lane == N4 - 1

    def shifted(x, by):
        return pltpu.roll(x, by % width, 1)

    def after(x):
        return jnp.where(final_lane, shifted(x, N4 - 1), shifted(x, -1))

    def before(x):
        return jnp.where(first_lane, shifted(x, 1 - N4), shifted(x, 1))

    chosen_rows = [profile(q) for q in range(-1, planes + 1)]
    for q in range(planes):
        low, mid, high = chosen_rows[q : q + 3]
        wide = jnp.broadcast_to(mid, (8, width))

        def pair(x):
            return (wide + x)[0:1]

        kinds = [
            w[0] * (mid + low),
            w[0] * (mid + high),
            w[2] * pair(shifted(wide, -N4)),
            w[2] * pair(shifted(wide, N4)),
            w[3] * pair(after(wide)),
            w[3] * pair(before(wide)),
            w[1] * mid,
        ]
        for k, row in enumerate(kinds):
            coefs[q, pl.ds(k, 1), :] = row
    gain = jnp.broadcast_to(row_gain[...], (128, rows))
    gains[0] = jnp.transpose(gain)
    gains[1] = jnp.transpose(gain + pltpu.roll(gain, rows - 1, 1))
    gains[2] = jnp.transpose(gain + pltpu.roll(gain, 1, 1))

    for load in loads:
        load.wait()

    def column(k, where):
        return jnp.concatenate([gains[k, where, :]] * (width // 128), axis=1)

    def diffuse(q, i):
        start = pl.multiple_of(i * STEP, STEP)
        here = pl.ds(start, STEP)
        inner = pl.ds(pl.multiple_of(start + PAD, 8), STEP)
        block = u[q, pl.ds(start, STEP + 2 * PAD), :]
        center = block[PAD : PAD + STEP]
        up = block[PAD - 1 : PAD - 1 + STEP]
        down = block[PAD + 1 : PAD + 1 + STEP]
        lower = u[jnp.maximum(q - 1, 0), inner, :]
        upper = u[jnp.minimum(q + 1, planes - 1), inner, :]

        def k(index):
            return coefs[q, pl.ds(index, 1), :]

        flow = k(0) * (lower - center) + k(1) * (upper - center)
        flow = flow + k(2) * (shifted(center, -N4) - center)
        flow = flow + k(3) * (shifted(center, N4) - center)
        flow = flow + k(4) * (after(center) - center) + k(5) * (before(center) - center)
        along = column(1, here) * (down - center) + column(2, here) * (up - center)
        diffused[q, here, :] = center + column(0, here) * flow + k(6) * along

    def join(q, c, index, other):
        def body(i, carry):
            start = pl.multiple_of(c * chunk + i * STEP, STEP)
            here = pl.ds(start, STEP)
            center = u[q, pl.ds(pl.multiple_of(start + PAD, 8), STEP), :]
            change = coefs[q, pl.ds(index, 1), :] * (other[here, :] - center)
            diffused[q, here, :] = diffused[q, here, :] + column(0, here) * change
            return carry

        lax.fori_loop(0, chunk // STEP, body, 0, unroll=True)

    def lift_lanes(q, c):
        where = at(c)
        total_ = jnp.zeros((chunk, width), jnp.float32)
        for part in reversed(three_parts(diffused[q, where, :])):
            total_ = total_ + jnp.dot(
                part, merged_table[...], preferred_element_type=jnp.float32
            )
        for k, part in enumerate(three_parts(total_)):
            parts[k, where, :] = part

    def lift_rows(q):
        block = min(128, rows)

        def body(i, carry):
            where = pl.ds(pl.multiple_of(i * block, block), block)
            table = second_table[where, :]
            total_ = jnp.dot(table, parts[2], preferred_element_type=jnp.float32)
            total_ = total_ + jnp.dot(table, parts[1], preferred_element_type=jnp.float32)
            total_ = total_ + jnp.dot(table, parts[0], preferred_element_type=jnp.float32)
            lifted[q, where, :] = total_
            return carry

        lax.fori_loop(0, rows // block, body, 0)

    def base(j, carry):
        diffuse(j // (rows // STEP), j % (rows // STEP))
        return carry

    steps = planes * (rows // STEP)
    lax.fori_loop(0, steps, base, 0, unroll=2)

    def inner_plane(q, carry):
        each(lambda c: lift_lanes(q, c))
        lift_rows(q)
        return carry

    lax.fori_loop(1, planes - 1, inner_plane, 0)

    def first_arrived(c):
        last_plane(c).wait_recv()
        join(0, c, 0, f_prev)
        lift_lanes(0, c)

    each(first_arrived)
    lift_rows(0)

    def send(c):
        for holds, copy in sends:

            @pl.when(holds)
            def _(copy=copy):
                copy(c).start()

    each(send)

    def last_arrived(c):
        first_plane(c).wait_recv()
        join(planes - 1, c, 1, f_next)
        lift_lanes(planes - 1, c)

    each(last_arrived)
    lift_rows(planes - 1)

    def store(q, c):
        return pltpu.make_async_copy(
            result.at[q, at(c), :], out.at[q, at(c), :], out_sem.at[q, c]
        )

    for q in range(1, planes):
        s = low_bit(q)
        if q + s < planes:

            def whole(c, q=q, s=s):
                where = at(c)
                result[q, where, :] = lifted[q, where, :] - HALF * (
                    lifted[q - s, where, :] + lifted[q + s, where, :]
                )
                store(q, c).start()

            each(whole)

    def finish(c):
        where = at(c)
        to_behind(c).wait_recv()
        for q in range(1, planes):
            s = low_bit(q)
            if q + s == planes:
                result[q, where, :] = lifted[q, where, :] - HALF * (
                    lifted[q - s, where, :] + y_next[where, :]
                )
                store(q, c).start()

        @pl.when(odd)
        def _():
            result[0, where, :] = lifted[0, where, :] - HALF * (
                y_left[where, :] + y_next[where, :]
            )

        @pl.when(rank == n // 2)
        def _():
            to_pair(c).wait_recv()
            result[0, where, :] = lifted[0, where, :] - y_left[where, :]

        @pl.when(rank == 0)
        def _():
            result[0, where, :] = lifted[0, where, :]

        @pl.when(even & (rank % (n // 2) != 0))
        def _():
            if RELAY:

                @pl.when(jnp.logical_not(middle))
                def _():
                    to_pair(c).wait_recv()
                    own(c, y_right, 2, 4, ahead).wait_recv()

            else:
                to_pair(c).wait_recv()
                own(c, y_right, 2, 4, ahead).wait_recv()
            result[0, where, :] = lifted[0, where, :] - HALF * (
                y_left[where, :] + y_right[where, :]
            )

        store(0, c).start()

    def pass_on(c):
        @pl.when(odd)
        def _():
            to_pair(c).wait_recv()
            relay(c).start()

        if RELAY:

            @pl.when(middle)
            def _():
                to_pair(c).wait_recv()
                to_opposite(c).start()
                own(c, y_right, 2, 4, ahead).wait_recv()
                to_coarse(c).start()

    pass_on(0)

    def turn(c, carry):
        pass_on(c)
        finish(c - 1)
        return carry

    lax.fori_loop(1, CHUNKS, turn, 0)
    finish(CHUNKS - 1)

    each(lambda c: last_plane(c).wait_send())
    each(lambda c: first_plane(c).wait_send())
    for holds, copy in [*sends, (odd, relay), *([(middle, to_coarse), (middle, to_opposite)] if RELAY else [])]:

        @pl.when(holds)
        def _(copy=copy):
            each(lambda c: copy(c).wait_send())

    for q in range(planes):
        each(lambda c, q=q: store(q, c).wait())


def on_device(field, selector, profiles, row_gain, levels):
    planes, rows, width = field.shape
    n = lax.axis_size("split")
    kinds = 4 + 2 * n.bit_length()
    plane = pltpu.VMEM((rows, width), jnp.float32)
    block = pltpu.VMEM((planes, rows, width), jnp.float32)
    return pl.pallas_call(
        functools.partial(kernel, n),
        out_shape=jax.ShapeDtypeStruct(field.shape, jnp.float32),
        in_specs=[
            pl.BlockSpec(memory_space=pl.ANY),
            pl.BlockSpec(memory_space=pltpu.SMEM),
            pl.BlockSpec(memory_space=pltpu.VMEM),
            pl.BlockSpec(memory_space=pltpu.VMEM),
            pl.BlockSpec(memory_space=pltpu.SMEM),
        ],
        out_specs=pl.BlockSpec(memory_space=pl.ANY),
        scratch_shapes=[
            pltpu.VMEM((planes, rows + 2 * PAD, width), jnp.float32),
            block,
            pltpu.VMEM((3, rows, width), jnp.bfloat16),
            block,
            block,
            plane,
            plane,
            plane,
            plane,
            plane,
            pltpu.VMEM((planes, 8, width), jnp.float32),
            pltpu.VMEM((3, rows, 128), jnp.float32),
            pltpu.VMEM((rows, rows), jnp.bfloat16),
            pltpu.VMEM((width, width), jnp.bfloat16),
            pltpu.SemaphoreType.DMA((3,)),
            pltpu.SemaphoreType.DMA((kinds, CHUNKS)),
            pltpu.SemaphoreType.DMA((5, CHUNKS)),
            pltpu.SemaphoreType.DMA((planes, CHUNKS)),
        ],
        compiler_params=pltpu.CompilerParams(
            collective_id=0, has_side_effects=True, vmem_limit_bytes=LIMIT * 1024 * 1024
        ),
        name="step_and_lift",
    )(
        field,
        selector,
        profiles,
        row_gain.reshape(1, rows),
        levels,
    )


def solution(mesh):
    placed = (
        P(("group", "split"), None, None),
        P("group"),
        P("group", None),
        P("group"),
        P("group"),
    )
    return jax.shard_map(
        on_device,
        mesh=mesh,
        in_specs=placed,
        out_specs=P(("group", "split"), None, None),
        check_vma=False,
    )
```
